32 devices in a mesh: node: 4 (over z), drow: 4 (over x, core), dcol: 2 (over y).
Axes of the slice: x: 2, y: 2, z: 4, core: 2. Of those that a mesh axis runs over, the one named last changes fastest.
Arguments:
- freq_resp: bfloat16 [2, 8, 4096, 4096], P(None, None, ('drow', 'dcol'), 'node'), may hold values from -0.09375 to 0.09375
- node_coords: int32 [2, 4096], P(None, 'node'), may hold values from 0 to 1023
- heading_steps: int32 [2, 512], replicated, may hold values from -8 to 8
- spectral_weights: int32 [8, 512], replicated, may hold values from 1 to 64
Outputs:
- cross_spectra: float32 [2, 8, 4, 1024, 4096], P(None, None, 'drow', 'node', 'dcol')
The draws below stay inside these ranges and needn't reach their ends.
All inputs are finite; a program needn't handle non-finite values.
Results may differ from the reference program's by a relative error of at most 0.0038.
Values may be sent and summed in bfloat16 or wider, within the bound.
A program may use at most 192 MiB of HBM per device.

```python
import math
import jax
import jax.numpy as jnp

DOF = 4096
DIRS = 512
FREQS = 8
GRID = 1024
NODES = 4096
N_NODE = 4
N_DROW = 4
N_DCOL = 2


def set_ends(array, stream_key, least, top_value):
    extent = array.shape
    spot = [jax.random.randint(jax.random.fold_in(stream_key, axis), (), 0, extent[axis]) for axis in range(len(extent))]
    array = array.at[tuple(spot)].set(least)
    longest = extent.index(max(extent))
    spot[longest] = (spot[longest] + 1) % extent[longest]
    return array.at[tuple(spot)].set(top_value)


def level_of(stream_key, shape, shards, least, largest):
    gain = 1.0
    for dim, parts in shards:
        steps = jax.random.uniform(jax.random.fold_in(jax.random.fold_in(stream_key, 6), dim), (parts,), jnp.float32, least / len(shards), largest / len(shards))
        gain = gain * jnp.repeat(jnp.exp(steps), shape[dim] // parts).reshape((-1,) + (1,) * (len(shape) - 1 - dim))
    return gain


def scatter_about(rng, extent, scale, reach, cuts=(), held_as=jnp.bfloat16):
    loudness = level_of(rng, extent, cuts, -0.22, 0.18) if cuts else 1.0
    array = jax.random.normal(rng, extent, jnp.float32) * scale * loudness
    return jnp.minimum(jnp.maximum(array, -reach), reach).astype(held_as)


def setup_inputs(seed: int = 0) -> dict:
    arg_keys = jax.random.split(jax.random.key(seed), 5)
    freq_resp = scatter_about(arg_keys[0], (2, FREQS, DOF, NODES), NODES ** -0.5, 0.09375, ((2, 8), (3, 4)))
    node_coords = set_ends(jax.random.randint(arg_keys[1], (2, NODES), 0, GRID), jax.random.fold_in(arg_keys[1], 1), 0, GRID - 1).astype(jnp.int32)
    heading_steps = set_ends(jax.random.randint(arg_keys[2], (2, DIRS), -8, 9), jax.random.fold_in(arg_keys[2], 1), -8, 8).astype(jnp.int32)
    spectral_weights = set_ends(jax.random.randint(arg_keys[3], (FREQS, DIRS), 1, 65), jax.random.fold_in(arg_keys[3], 1), 1, 64).astype(jnp.int32)
    return {"freq_resp": freq_resp, "node_coords": node_coords, "heading_steps": heading_steps, "spectral_weights": spectral_weights}


def excitation(coords, heading_steps, spectral_weights):
    freq_index = (jnp.arange(FREQS, dtype=jnp.int32) + 1)[:, None, None]
    project = coords[0][:, None] * heading_steps[0][None, :] + coords[1][:, None] * heading_steps[1][None, :]
    turn_count = jnp.mod(freq_index * project[None], GRID)
    phase_angle = turn_count.astype(jnp.float32) * (2.0 * math.pi / GRID)
    spread = jnp.sqrt(spectral_weights.astype(jnp.float32) / (64.0 * DIRS))[:, None, :]
    load_re = (spread * jnp.cos(phase_angle)).astype(jnp.bfloat16)
    load_im = (-spread * jnp.sin(phase_angle)).astype(jnp.bfloat16)
    return (load_re, load_im)

def row_order(matrix):
    slice_rows = DOF // (N_DROW * N_DCOL * N_NODE)
    shaped = matrix.reshape(N_DROW, N_DCOL, N_NODE, slice_rows, DIRS)
    return shaped.transpose(0, 2, 1, 3, 4).reshape(DOF, DIRS)

def col_order(matrix):
    slice_rows = DOF // (N_DROW * N_DCOL * N_NODE)
    shaped = matrix.reshape(N_DROW, N_DCOL, N_NODE, slice_rows, DIRS)
    return shaped.transpose(1, 2, 0, 3, 4).reshape(DOF, DIRS)

def reference(freq_resp, node_coords, heading_steps, spectral_weights):
    load_re, load_im = excitation(node_coords, heading_steps, spectral_weights)
    results = []
    for freq_index in range(FREQS):
        resp_re = freq_resp[0, freq_index]
        resp_im = freq_resp[1, freq_index]
        amp_re = (jnp.dot(resp_re, load_re[freq_index], preferred_element_type=jnp.float32) - jnp.dot(resp_im, load_im[freq_index], preferred_element_type=jnp.float32)).astype(jnp.bfloat16)
        amp_im = (jnp.dot(resp_re, load_im[freq_index], preferred_element_type=jnp.float32) + jnp.dot(resp_im, load_re[freq_index], preferred_element_type=jnp.float32)).astype(jnp.bfloat16)
        row_re = row_order(amp_re)
        row_im = row_order(amp_im)
        col_re = col_order(amp_re)
        col_im = col_order(amp_im)
        spec_re = jnp.dot(row_re, col_re.T, preferred_element_type=jnp.float32) + jnp.dot(row_im, col_im.T, preferred_element_type=jnp.float32)
        spec_im = jnp.dot(row_im, col_re.T, preferred_element_type=jnp.float32) - jnp.dot(row_re, col_im.T, preferred_element_type=jnp.float32)
        results.append(jnp.stack([spec_re, spec_im]))
    stacked = jnp.stack(results, axis=1)
    return stacked.reshape(2, FREQS, N_DROW, DOF // N_DROW, DOF)
```

```python
import functools
import math

import jax
import jax.numpy as jnp
from jax import lax
from jax.experimental import pallas as pl
from jax.experimental.pallas import tpu as pltpu
from jax.sharding import PartitionSpec as P

GRID = 1024
MIB = 1024 * 1024
MESH = pl.DeviceIdType.MESH


def unit_phase(turn):
    quarter = (turn + GRID // 8) >> 8
    rest = (turn - quarter * (GRID // 4)).astype(jnp.float32)
    x = rest * (2.0 * math.pi / GRID)
    x2 = x * x
    s = x * (1.0 + x2 * (-1.0 / 6 + x2 * (1.0 / 120 + x2 * (-1.0 / 5040 + x2 * (1.0 / 362880)))))
    c = 1.0 + x2 * (-0.5 + x2 * (1.0 / 24 + x2 * (-1.0 / 720 + x2 * (1.0 / 40320))))
    odd = (quarter & 1) == 1
    cos = jnp.where(odd, s, c)
    sin = jnp.where(odd, c, s)
    q = quarter & 3
    cos = jnp.where((q == 1) | (q == 2), -cos, cos)
    sin = jnp.where(q >= 2, -sin, sin)
    return cos, sin


def amp_kernel(coords_ref, steps_ref, weight_ref, h_ref, out_ref, c1, s1, cf, sf):
    nodes, dirs = c1.shape
    f = pl.program_id(0)

    @pl.when(f == 0)
    def _():
        project = (
            coords_ref[:, 0:1] * steps_ref[0:1, :] + coords_ref[:, 1:2] * steps_ref[1:2, :]
        )
        cos, sin = unit_phase(project & (GRID - 1))
        c1[...] = cos
        s1[...] = sin
        cf[...] = cos
        sf[...] = sin

    @pl.when(f > 0)
    def _():
        c, s = cf[...], sf[...]
        cf[...] = c * c1[...] - s * s1[...]
        sf[...] = s * c1[...] + c * s1[...]

    w = weight_ref[0]
    load_re = (w * cf[...]).astype(jnp.bfloat16)
    load_im = (-w * sf[...]).astype(jnp.bfloat16)
    h_re, h_im = h_ref[0, 0], h_ref[1, 0]
    dot = functools.partial(jnp.dot, preferred_element_type=jnp.float32)
    out_ref[0, :, :dirs] = (dot(h_re, load_re) - dot(h_im, load_im)).astype(jnp.bfloat16)
    out_ref[0, :, dirs:] = (dot(h_re, load_im) + dot(h_im, load_re)).astype(jnp.bfloat16)


def share_kernel(
    n_node, n_dcol, part, col_ref, row_ref, up, down, piece,
    up_s, up_r, dn_s, dn_r, zu_s, zd_s, z_r, x_s, x_r, c_s, c_r, y_s, y_r, loc,
):
    freqs = part.shape[0]
    n = lax.axis_index("node")
    r = lax.axis_index("drow")
    c = lax.axis_index("dcol")
    rx = (r + 2) % 4
    rc = r + 1 - 2 * (r % 2)
    far = rc + 2 - 4 * (rc // 2)
    above, below = {"node": n + 1}, {"node": n - 1}
    has_up, has_dn = n < n_node - 1, n > 0

    def remote(src, dst, send, recv, where):
        return pltpu.make_async_remote_copy(
            src_ref=src, dst_ref=dst, send_sem=send, recv_sem=recv,
            device_id=where, device_id_type=MESH,
        )

    def other(k):
        return (c + k) % n_dcol

    barrier = pltpu.get_barrier_semaphore()

    def greet(where):
        pl.semaphore_signal(barrier, inc=1, device_id=where, device_id_type=MESH)

    pl.when(has_up)(lambda: greet(above))
    pl.when(has_dn)(lambda: greet(below))
    greet({"drow": rx})
    greet({"drow": rc})
    for k in range(1, n_dcol):
        greet({"dcol": other(k)})
    peers = 1 + n_dcol + has_up.astype(jnp.int32) + has_dn.astype(jnp.int32)
    pl.semaphore_wait(barrier, peers)

    def hop_up(f, t, src):
        return remote(src.at[f, t], up.at[f, t], up_s.at[f, t], up_r.at[f, t], above)

    def hop_dn(f, t, src):
        return remote(src.at[f, t], down.at[f, t], dn_s.at[f, t], dn_r.at[f, t], below)

    def add(buf, f, t):
        buf[f, t] = (
            buf[f, t].astype(jnp.float32) + part[f, t].astype(jnp.float32)
        ).astype(jnp.bfloat16)

    def z_up(f, s, src):
        return remote(src, col_ref.at[f, s, r], zu_s.at[f, s], z_r.at[f, s], above)

    def z_dn(f, s, src):
        return remote(src, col_ref.at[f, s, r], zd_s.at[f, s], z_r.at[f, s], below)

    def to_x(f, s, src):
        return remote(src, col_ref.at[f, s, r], x_s.at[f, s], x_r.at[f, s], {"drow": rx})

    def to_core(f, s, q, src):
        row = r if q == 0 else rx
        return remote(
            src, col_ref.at[f, s, row], c_s.at[f, q, s], c_r.at[f, q, s], {"drow": rc}
        )

    def to_y(f, k):
        return remote(
            piece.at[f], row_ref.at[f, c], y_s.at[f, k], y_r.at[f, k], {"dcol": other(k)}
        )

    def own_col(f):
        return pltpu.make_async_copy(piece.at[f], col_ref.at[f, n, r], loc.at[f, 0])

    def own_row(f):
        return pltpu.make_async_copy(piece.at[f], row_ref.at[f, c], loc.at[f, 1])

    def hops(f):
        for k in range(n_node - 1):
            t = n_node - 1 - k

            @pl.when((t > n) & (n == 0))
            def _():
                hop_up(f, t, part).start()

            @pl.when((t > n) & (n > 0))
            def _():
                hop_up(f, t, up).wait_recv()
                add(up, f, t)
                hop_up(f, t, up).start()

            t2 = k

            @pl.when((t2 < n) & (n == n_node - 1))
            def _():
                hop_dn(f, t2, part).start()

            @pl.when((t2 < n) & (n < n_node - 1))
            def _():
                hop_dn(f, t2, down).wait_recv()
                add(down, f, t2)
                hop_dn(f, t2, down).start()

    def finish(f):
        @pl.when(has_dn)
        def _():
            hop_up(f, n, up).wait_recv()

        @pl.when(has_up)
        def _():
            hop_dn(f, n, down).wait_recv()

        own = part[f, n].astype(jnp.float32)

        @pl.when(n == 0)
        def _():
            piece[f] = (own + down[f, n].astype(jnp.float32)).astype(jnp.bfloat16)

        @pl.when(n == n_node - 1)
        def _():
            piece[f] = (own + up[f, n].astype(jnp.float32)).astype(jnp.bfloat16)

        @pl.when(has_up & has_dn)
        def _():
            piece[f] = (
                own + up[f, n].astype(jnp.float32) + down[f, n].astype(jnp.float32)
            ).astype(jnp.bfloat16)

        src = piece.at[f]
        pl.when(has_up)(lambda: z_up(f, n, src).start())
        pl.when(has_dn)(lambda: z_dn(f, n, src).start())
        to_x(f, n, src).start()
        to_core(f, n, 0, src).start()
        for k in range(1, n_dcol):
            to_y(f, k).start()
        own_col(f).start()
        own_row(f).start()

    def spread(f):
        for d in range(1, n_node):
            lo, hi = n - d, n + d

            @pl.when(lo >= 0)
            def _():
                src = col_ref.at[f, lo, r]
                z_up(f, lo, src).wait_recv()
                pl.when(has_up)(lambda: z_up(f, lo, src).start())
                to_x(f, lo, src).start()
                to_core(f, lo, 0, src).start()

            @pl.when(hi < n_node)
            def _():
                src = col_ref.at[f, hi, r]
                z_dn(f, hi, src).wait_recv()
                pl.when(has_dn)(lambda: z_dn(f, hi, src).start())
                to_x(f, hi, src).start()
                to_core(f, hi, 0, src).start()

    def crossed(f):
        for s in range(n_node):
            src = col_ref.at[f, s, rx]
            remote(src, src, x_s.at[f, s], x_r.at[f, s], {"drow": rx}).wait_recv()
            to_core(f, s, 1, src).start()

    def settle(f):
        src = piece.at[f]
        own_col(f).wait()
        own_row(f).wait()
        for k in range(1, n_dcol):
            to_y(f, k).wait_send()
            to_y(f, k).wait_recv()
        for s in range(n_node):
            to_x(f, s, src).wait_send()
            for q in range(2):
                dst = col_ref.at[f, s, rc if q == 0 else far]
                to_core(f, s, q, src).wait_send()
                remote(
                    dst, dst, c_s.at[f, q, s], c_r.at[f, q, s], {"drow": rc}
                ).wait_recv()

            pl.when(has_up & (n >= s))(lambda: z_up(f, s, src).wait_send())
            pl.when(has_dn & (n <= s))(lambda: z_dn(f, s, src).wait_send())
            pl.when(s > n)(lambda: hop_up(f, s, part).wait_send())
            pl.when(s < n)(lambda: hop_dn(f, s, part).wait_send())

    @pl.loop(0, freqs + 3)
    def _(i):
        pl.when(i < freqs)(lambda: hops(i))
        pl.when((i >= 1) & (i < freqs + 1))(lambda: finish(i - 1))
        pl.when((i >= 2) & (i < freqs + 2))(lambda: spread(i - 2))
        pl.when(i >= 3)(lambda: crossed(i - 3))

    @pl.loop(0, freqs)
    def _(f):
        settle(f)


def spec_kernel(row_ref, col_ref, out_ref):
    row = row_ref[0]
    half = row.shape[1] // 2
    turned = jnp.concatenate([row[:, half:], -row[:, :half]], axis=1)
    col = col_ref[0]
    dims = (((1,), (1,)), ((), ()))
    out_ref[0, 0, 0] = lax.dot_general(row, col, dims, preferred_element_type=jnp.float32)
    out_ref[1, 0, 0] = lax.dot_general(turned, col, dims, preferred_element_type=jnp.float32)


def local(n_node, n_drow, n_dcol, freq_resp, node_coords, heading_steps, spectral_weights):
    _, freqs, dofs, nodes = freq_resp.shape
    dirs = heading_steps.shape[1]
    width = 2 * dirs
    rows = dofs // n_node
    weight = jnp.sqrt(spectral_weights.astype(jnp.float32) / (64.0 * 512))[:, None, :]
    part = pl.pallas_call(
        amp_kernel,
        out_shape=jax.ShapeDtypeStruct((freqs, dofs, width), jnp.bfloat16),
        grid=(freqs,),
        in_specs=[
            pl.BlockSpec((nodes, 2), lambda f: (0, 0)),
            pl.BlockSpec((2, dirs), lambda f: (0, 0)),
            pl.BlockSpec((1, 1, dirs), lambda f: (f, 0, 0)),
            pl.BlockSpec((2, 1, dofs, nodes), lambda f: (0, f, 0, 0)),
        ],
        out_specs=pl.BlockSpec((1, dofs, width), lambda f: (f, 0, 0)),
        scratch_shapes=[pltpu.VMEM((nodes, dirs), jnp.float32)] * 4,
        compiler_params=pltpu.CompilerParams(vmem_limit_bytes=48 * MIB),
    )(node_coords.T, heading_steps, weight, freq_resp)
    part = part.reshape(freqs, n_node, rows, width)

    dma = pltpu.SemaphoreType.DMA
    fn = (freqs, n_node)
    col, row = pl.pallas_call(
        functools.partial(share_kernel, n_node, n_dcol),
        out_shape=(
            jax.ShapeDtypeStruct((freqs, n_node, n_drow, rows, width), jnp.bfloat16),
            jax.ShapeDtypeStruct((freqs, n_dcol, rows, width), jnp.bfloat16),
        ),
        in_specs=[pl.BlockSpec(memory_space=pltpu.VMEM)],
        out_specs=[pl.BlockSpec(memory_space=pl.ANY)] * 2,
        scratch_shapes=[
            pltpu.VMEM((freqs, n_node, rows, width), jnp.bfloat16),
            pltpu.VMEM((freqs, n_node, rows, width), jnp.bfloat16),
            pltpu.VMEM((freqs, rows, width), jnp.bfloat16),
            dma(fn), dma(fn), dma(fn), dma(fn),
            dma(fn), dma(fn), dma(fn),
            dma(fn), dma(fn),
            dma((freqs, 2, n_node)), dma((freqs, 2, n_node)),
            dma((freqs, n_dcol)), dma((freqs, n_dcol)),
            dma((freqs, 2)),
        ],
        compiler_params=pltpu.CompilerParams(
            collective_id=0, has_side_effects=True, vmem_limit_bytes=48 * MIB
        ),
    )(part)
    col = col.reshape(freqs, n_node * n_drow * rows, width)
    row = row.reshape(freqs, n_dcol * rows, width)
    a, b = row.shape[1], col.shape[1]
    return pl.pallas_call(
        spec_kernel,
        out_shape=jax.ShapeDtypeStruct((2, freqs, 1, a, b), jnp.float32),
        grid=(freqs,),
        in_specs=[
            pl.BlockSpec((1, a, width), lambda f: (f, 0, 0)),
            pl.BlockSpec((1, b, width), lambda f: (f, 0, 0)),
        ],
        out_specs=pl.BlockSpec((2, 1, 1, a, b), lambda f: (0, f, 0, 0, 0)),
        compiler_params=pltpu.CompilerParams(vmem_limit_bytes=48 * MIB),
    )(row, col)


def solution(mesh):
    sizes = (mesh.shape["node"], mesh.shape["drow"], mesh.shape["dcol"])
    placed = (P(None, None, ("drow", "dcol"), "node"), P(None, "node"), P(), P())
    return jax.shard_map(
        functools.partial(local, *sizes),
        mesh=mesh,
        in_specs=placed,
        out_specs=P(None, None, "drow", "node", "dcol"),
        check_vma=False,
    )
```

```python
import functools
import math

import jax
import jax.numpy as jnp
from jax import lax
from jax.experimental import pallas as pl
from jax.experimental.pallas import tpu as pltpu
from jax.sharding import PartitionSpec as P

GRID = 1024
MIB = 1024 * 1024
MESH = pl.DeviceIdType.MESH


def unit_phase(turn):
    quarter = (turn + GRID // 8) >> 8
    rest = (turn - quarter * (GRID // 4)).astype(jnp.float32)
    x = rest * (2.0 * math.pi / GRID)
    x2 = x * x
    s = x * (1.0 + x2 * (-1.0 / 6 + x2 * (1.0 / 120 + x2 * (-1.0 / 5040 + x2 * (1.0 / 362880)))))
    c = 1.0 + x2 * (-0.5 + x2 * (1.0 / 24 + x2 * (-1.0 / 720 + x2 * (1.0 / 40320))))
    odd = (quarter & 1) == 1
    cos = jnp.where(odd, s, c)
    sin = jnp.where(odd, c, s)
    q = quarter & 3
    cos = jnp.where((q == 1) | (q == 2), -cos, cos)
    sin = jnp.where(q >= 2, -sin, sin)
    return cos, sin


def amp_kernel(coords_ref, steps_ref, weight_ref, h_ref, out_ref, c1, s1, cf, sf):
    f = pl.program_id(0)

    @pl.when(f == 0)
    def _():
        project = (
            coords_ref[:, 0:1] * steps_ref[0:1, :] + coords_ref[:, 1:2] * steps_ref[1:2, :]
        )
        cos, sin = unit_phase(project & (GRID - 1))
        c1[...] = cos
        s1[...] = sin
        cf[...] = cos
        sf[...] = sin

    @pl.when(f > 0)
    def _():
        c, s = cf[...], sf[...]
        cf[...] = c * c1[...] - s * s1[...]
        sf[...] = s * c1[...] + c * s1[...]

    w = weight_ref[0]
    load_re = (w * cf[...]).astype(jnp.bfloat16)
    load_im = (-w * sf[...]).astype(jnp.bfloat16)
    h_re, h_im = h_ref[0, 0], h_ref[1, 0]
    dot = functools.partial(jnp.dot, preferred_element_type=jnp.float32)
    out_ref[0] = (dot(h_re, load_re) - dot(h_im, load_im)).astype(jnp.bfloat16)
    out_ref[1] = (dot(h_re, load_im) + dot(h_im, load_re)).astype(jnp.bfloat16)


def share_kernel(
    n_node, n_dcol, part, col_ref, row_ref, up, down, piece,
    up_s, up_r, dn_s, dn_r, zu_s, zd_s, z_r, x_s, x_r, c_s, c_r, y_s, y_r, loc,
):
    freqs = part.shape[0]
    n = lax.axis_index("node")
    r = lax.axis_index("drow")
    c = lax.axis_index("dcol")
    rx = (r + 2) % 4
    rc = r + 1 - 2 * (r % 2)
    far = rc + 2 - 4 * (rc // 2)
    above, below = {"node": n + 1}, {"node": n - 1}
    has_up, has_dn = n < n_node - 1, n > 0

    def remote(src, dst, send, recv, where):
        return pltpu.make_async_remote_copy(
            src_ref=src, dst_ref=dst, send_sem=send, recv_sem=recv,
            device_id=where, device_id_type=MESH,
        )

    def other(k):
        return (c + k) % n_dcol

    barrier = pltpu.get_barrier_semaphore()

    def greet(where):
        pl.semaphore_signal(barrier, inc=1, device_id=where, device_id_type=MESH)

    pl.when(has_up)(lambda: greet(above))
    pl.when(has_dn)(lambda: greet(below))
    greet({"drow": rx})
    greet({"drow": rc})
    for k in range(1, n_dcol):
        greet({"dcol": other(k)})
    peers = 1 + n_dcol + has_up.astype(jnp.int32) + has_dn.astype(jnp.int32)
    pl.semaphore_wait(barrier, peers)

    def hop_up(f, t, src):
        return remote(src.at[f, t], up.at[f, t], up_s.at[f, t], up_r.at[f, t], above)

    def hop_dn(f, t, src):
        return remote(src.at[f, t], down.at[f, t], dn_s.at[f, t], dn_r.at[f, t], below)

    def add(buf, f, t):
        buf[f, t] = (
            buf[f, t].astype(jnp.float32) + part[f, t].astype(jnp.float32)
        ).astype(jnp.bfloat16)

    def z_up(f, s, src):
        return remote(src, col_ref.at[f, s, r], zu_s.at[f, s], z_r.at[f, s], above)

    def z_dn(f, s, src):
        return remote(src, col_ref.at[f, s, r], zd_s.at[f, s], z_r.at[f, s], below)

    def to_x(f, s, src):
        return remote(src, col_ref.at[f, s, r], x_s.at[f, s], x_r.at[f, s], {"drow": rx})

    def to_core(f, s, q, src):
        row = r if q == 0 else rx
        return remote(
            src, col_ref.at[f, s, row], c_s.at[f, q, s], c_r.at[f, q, s], {"drow": rc}
        )

    def to_y(f, k):
        return remote(
            piece.at[f], row_ref.at[f, c], y_s.at[f, k], y_r.at[f, k], {"dcol": other(k)}
        )

    def own_col(f):
        return pltpu.make_async_copy(piece.at[f], col_ref.at[f, n, r], loc.at[f, 0])

    def own_row(f):
        return pltpu.make_async_copy(piece.at[f], row_ref.at[f, c], loc.at[f, 1])

    def hops(f):
        for k in range(n_node - 1):
            t = n_node - 1 - k

            @pl.when((t > n) & (n == 0))
            def _():
                hop_up(f, t, part).start()

            @pl.when((t > n) & (n > 0))
            def _():
                hop_up(f, t, up).wait_recv()
                add(up, f, t)
                hop_up(f, t, up).start()

            t2 = k

            @pl.when((t2 < n) & (n == n_node - 1))
            def _():
                hop_dn(f, t2, part).start()

            @pl.when((t2 < n) & (n < n_node - 1))
            def _():
                hop_dn(f, t2, down).wait_recv()
                add(down, f, t2)
                hop_dn(f, t2, down).start()

    def finish(f):
        @pl.when(has_dn)
        def _():
            hop_up(f, n, up).wait_recv()

        @pl.when(has_up)
        def _():
            hop_dn(f, n, down).wait_recv()

        own = part[f, n].astype(jnp.float32)

        @pl.when(n == 0)
        def _():
            piece[f] = (own + down[f, n].astype(jnp.float32)).astype(jnp.bfloat16)

        @pl.when(n == n_node - 1)
        def _():
            piece[f] = (own + up[f, n].astype(jnp.float32)).astype(jnp.bfloat16)

        @pl.when(has_up & has_dn)
        def _():
            piece[f] = (
                own + up[f, n].astype(jnp.float32) + down[f, n].astype(jnp.float32)
            ).astype(jnp.bfloat16)

        src = piece.at[f]
        pl.when(has_up)(lambda: z_up(f, n, src).start())
        pl.when(has_dn)(lambda: z_dn(f, n, src).start())
        to_x(f, n, src).start()
        to_core(f, n, 0, src).start()
        for k in range(1, n_dcol):
            to_y(f, k).start()
        own_col(f).start()
        own_row(f).start()

    def spread(f):
        for d in range(1, n_node):
            lo, hi = n - d, n + d

            @pl.when(lo >= 0)
            def _():
                src = col_ref.at[f, lo, r]
                z_up(f, lo, src).wait_recv()
                pl.when(has_up)(lambda: z_up(f, lo, src).start())
                to_x(f, lo, src).start()
                to_core(f, lo, 0, src).start()

            @pl.when(hi < n_node)
            def _():
                src = col_ref.at[f, hi, r]
                z_dn(f, hi, src).wait_recv()
                pl.when(has_dn)(lambda: z_dn(f, hi, src).start())
                to_x(f, hi, src).start()
                to_core(f, hi, 0, src).start()

    def crossed(f):
        for s in range(n_node):
            src = col_ref.at[f, s, rx]
            remote(src, src, x_s.at[f, s], x_r.at[f, s], {"drow": rx}).wait_recv()
            to_core(f, s, 1, src).start()

    def settle(f):
        src = piece.at[f]
        own_col(f).wait()
        own_row(f).wait()
        for k in range(1, n_dcol):
            to_y(f, k).wait_send()
            to_y(f, k).wait_recv()
        for s in range(n_node):
            to_x(f, s, src).wait_send()
            for q in range(2):
                dst = col_ref.at[f, s, rc if q == 0 else far]
                to_core(f, s, q, src).wait_send()
                remote(
                    dst, dst, c_s.at[f, q, s], c_r.at[f, q, s], {"drow": rc}
                ).wait_recv()

            pl.when(has_up & (n >= s))(lambda: z_up(f, s, src).wait_send())
            pl.when(has_dn & (n <= s))(lambda: z_dn(f, s, src).wait_send())
            pl.when(s > n)(lambda: hop_up(f, s, part).wait_send())
            pl.when(s < n)(lambda: hop_dn(f, s, part).wait_send())

    @pl.loop(0, freqs + 3)
    def _(i):
        pl.when(i < freqs)(lambda: hops(i))
        pl.when((i >= 1) & (i < freqs + 1))(lambda: finish(i - 1))
        pl.when((i >= 2) & (i < freqs + 2))(lambda: spread(i - 2))
        pl.when(i >= 3)(lambda: crossed(i - 3))

    @pl.loop(0, freqs)
    def _(f):
        settle(f)


def spec_kernel(row_ref, col_ref, out_ref):
    dims = (((1,), (1,)), ((), ()))

    def dot(p, q):
        return lax.dot_general(row_ref[p], col_ref[q], dims, preferred_element_type=jnp.float32)

    out_ref[0, 0, 0] = dot(0, 0) + dot(1, 1)
    out_ref[1, 0, 0] = dot(1, 0) - dot(0, 1)


def local(n_node, n_drow, n_dcol, freq_resp, node_coords, heading_steps, spectral_weights):
    _, freqs, dofs, nodes = freq_resp.shape
    dirs = heading_steps.shape[1]
    width, chunks = dirs, 2 * freqs
    rows = dofs // n_node
    weight = jnp.sqrt(spectral_weights.astype(jnp.float32) / (64.0 * 512))[:, None, :]
    part = pl.pallas_call(
        amp_kernel,
        out_shape=jax.ShapeDtypeStruct((chunks, dofs, width), jnp.bfloat16),
        grid=(freqs,),
        in_specs=[
            pl.BlockSpec((nodes, 2), lambda f: (0, 0)),
            pl.BlockSpec((2, dirs), lambda f: (0, 0)),
            pl.BlockSpec((1, 1, dirs), lambda f: (f, 0, 0)),
            pl.BlockSpec((2, 1, dofs, nodes), lambda f: (0, f, 0, 0)),
        ],
        out_specs=pl.BlockSpec((2, dofs, width), lambda f: (f, 0, 0)),
        scratch_shapes=[pltpu.VMEM((nodes, dirs), jnp.float32)] * 4,
        compiler_params=pltpu.CompilerParams(vmem_limit_bytes=48 * MIB),
    )(node_coords.T, heading_steps, weight, freq_resp)
    part = part.reshape(chunks, n_node, rows, width)

    dma = pltpu.SemaphoreType.DMA
    fn = (chunks, n_node)
    col, row = pl.pallas_call(
        functools.partial(share_kernel, n_node, n_dcol),
        out_shape=(
            jax.ShapeDtypeStruct((chunks, n_node, n_drow, rows, width), jnp.bfloat16),
            jax.ShapeDtypeStruct((chunks, n_dcol, rows, width), jnp.bfloat16),
        ),
        in_specs=[pl.BlockSpec(memory_space=pltpu.VMEM)],
        out_specs=[pl.BlockSpec(memory_space=pl.ANY)] * 2,
        scratch_shapes=[
            pltpu.VMEM((chunks, n_node, rows, width), jnp.bfloat16),
            pltpu.VMEM((chunks, n_node, rows, width), jnp.bfloat16),
            pltpu.VMEM((chunks, rows, width), jnp.bfloat16),
            dma(fn), dma(fn), dma(fn), dma(fn),
            dma(fn), dma(fn), dma(fn),
            dma(fn), dma(fn),
            dma((chunks, 2, n_node)), dma((chunks, 2, n_node)),
            dma((chunks, n_dcol)), dma((chunks, n_dcol)),
            dma((chunks, 2)),
        ],
        compiler_params=pltpu.CompilerParams(
            collective_id=0, has_side_effects=True, vmem_limit_bytes=48 * MIB
        ),
    )(part)
    col = col.reshape(chunks, n_node * n_drow * rows, width)
    row = row.reshape(chunks, n_dcol * rows, width)
    a, b = row.shape[1], col.shape[1]
    return pl.pallas_call(
        spec_kernel,
        out_shape=jax.ShapeDtypeStruct((2, freqs, 1, a, b), jnp.float32),
        grid=(freqs,),
        in_specs=[
            pl.BlockSpec((2, a, width), lambda f: (f, 0, 0)),
            pl.BlockSpec((2, b, width), lambda f: (f, 0, 0)),
        ],
        out_specs=pl.BlockSpec((2, 1, 1, a, b), lambda f: (0, f, 0, 0, 0)),
        compiler_params=pltpu.CompilerParams(vmem_limit_bytes=48 * MIB),
    )(row, col)


def solution(mesh):
    sizes = (mesh.shape["node"], mesh.shape["drow"], mesh.shape["dcol"])
    placed = (P(None, None, ("drow", "dcol"), "node"), P(None, "node"), P(), P())
    return jax.shard_map(
        functools.partial(local, *sizes),
        mesh=mesh,
        in_specs=placed,
        out_specs=P(None, None, "drow", "node", "dcol"),
        check_vma=False,
    )
```
